32 devices in a mesh: dp: 8 (over z, x), tensor: 4 (over y, core).
Axes of the slice: x: 2, y: 2, z: 4, core: 2. Of those that a mesh axis runs over, the one named last changes fastest.
Arguments:
- inputs: bfloat16 [8192, 2048], P(('dp', 'tensor')), may hold values from -6 to 6
- cotangent: bfloat16 [8192, 2048], P(('dp', 'tensor')), may hold values from -6 to 6
- qkv_weight: float32 [2048, 3, 2048], P('dp', None, 'tensor'), may hold values from -0.125 to 0.125
- qkv_first: float32 [2048, 3, 2048], P('dp', None, 'tensor'), may hold values from -64 to 64
- qkv_second: float32 [2048, 3, 2048], P('dp', None, 'tensor'), may hold values from 8.192 to 32.768
- dense_weight: float32 [2048, 2048], P('dp', 'tensor'), may hold values from -0.5 to 0.5
- dense_first: float32 [2048, 2048], P('dp', 'tensor'), may hold values from -4 to 4
- dense_second: float32 [2048, 2048], P('dp', 'tensor'), may hold values from 0.04 to 0.16
- up_weight: float32 [2048, 8192], P('dp', 'tensor'), may hold values from -0.125 to 0.125
- up_first: float32 [2048, 8192], P('dp', 'tensor'), may hold values from -16 to 16
- up_second: float32 [2048, 8192], P('dp', 'tensor'), may hold values from 0.73728 to 2.94912
- down_weight: float32 [2048, 8192], P('dp', 'tensor'), may hold values from -0.0625 to 0.0625
- down_first: float32 [2048, 8192], P('dp', 'tensor'), may hold values from -32 to 32
- down_second: float32 [2048, 8192], P('dp', 'tensor'), may hold values from 2.94912 to 11.79648
- qkv_bias: float32 [3, 2048], P(None, ('tensor', 'dp')), may hold values from -1.25 to 1.25
- qkv_bias_first: float32 [3, 2048], P(None, ('tensor', 'dp')), may hold values from -64 to 64
- qkv_bias_second: float32 [3, 2048], P(None, ('tensor', 'dp')), may hold values from 8.192 to 32.768
- up_bias: float32 [8192], P(('tensor', 'dp')), may hold values from -1.25 to 1.25
- up_bias_first: float32 [8192], P(('tensor', 'dp')), may hold values from -16 to 16
- up_bias_second: float32 [8192], P(('tensor', 'dp')), may hold values from 0.73728 to 2.94912
- norm_vectors: float32 [4, 2048], P(None, 'dp'), may hold values from -0.6 to 1.3, as said below
- norm_first: float32 [4, 2048], P(None, 'dp'), may hold values from -64 to 64
- norm_second: float32 [4, 2048], P(None, 'dp'), may hold values from 8.192 to 32.768
Outputs:
- output: bfloat16 [8192, 2048], P(('dp', 'tensor'))
- input_grad: float32 [8192, 2048], P(('dp', 'tensor'))
- qkv_grad: float32 [2048, 3, 2048], P('dp', None, 'tensor')
- qkv_new: float32 [2048, 3, 2048], P('dp', None, 'tensor')
- qkv_first_new: float32 [2048, 3, 2048], P('dp', None, 'tensor')
- qkv_second_new: float32 [2048, 3, 2048], P('dp', None, 'tensor')
- dense_grad: float32 [2048, 2048], P('dp', 'tensor')
- dense_new: float32 [2048, 2048], P('dp', 'tensor')
- dense_first_new: float32 [2048, 2048], P('dp', 'tensor')
- dense_second_new: float32 [2048, 2048], P('dp', 'tensor')
- up_grad: float32 [2048, 8192], P('dp', 'tensor')
- up_new: float32 [2048, 8192], P('dp', 'tensor')
- up_first_new: float32 [2048, 8192], P('dp', 'tensor')
- up_second_new: float32 [2048, 8192], P('dp', 'tensor')
- down_grad: float32 [2048, 8192], P('dp', 'tensor')
- down_new: float32 [2048, 8192], P('dp', 'tensor')
- down_first_new: float32 [2048, 8192], P('dp', 'tensor')
- down_second_new: float32 [2048, 8192], P('dp', 'tensor')
- qkv_bias_grad: float32 [3, 2048], P(None, ('tensor', 'dp'))
- qkv_bias_new: float32 [3, 2048], P(None, ('tensor', 'dp'))
- qkv_bias_first_new: float32 [3, 2048], P(None, ('tensor', 'dp'))
- qkv_bias_second_new: float32 [3, 2048], P(None, ('tensor', 'dp'))
- up_bias_grad: float32 [8192], P(('tensor', 'dp'))
- up_bias_new: float32 [8192], P(('tensor', 'dp'))
- up_bias_first_new: float32 [8192], P(('tensor', 'dp'))
- up_bias_second_new: float32 [8192], P(('tensor', 'dp'))
- norm_grad: float32 [4, 2048], P(None, 'dp')
- norm_new: float32 [4, 2048], P(None, 'dp')
- norm_first_new: float32 [4, 2048], P(None, 'dp')
- norm_second_new: float32 [4, 2048], P(None, 'dp')
The draws below stay inside these ranges and needn't reach their ends.
Inputs may be any that keep to these rules, and one draw needn't show every extreme that they name: `norm_vectors`: row 0 lies near 1, rows 1 to 3 near 0.
All inputs are finite; a program needn't handle non-finite values.
Results may differ from the reference program's by a relative error of at most 0.012.
The reference program's roundings to bfloat16 on the way count: a program that leaves them out, or rounds other values in their place, can miss the bound.
Values may be sent and summed in bfloat16 or wider, within the bound.
A program may use at most 256 MiB of HBM per device.

```python
import math
import jax
import jax.numpy as jnp
from jax import lax

D = 2048
HEADS = 32
HEAD = 64
ROT = 32
FF = 8192
LENGTH = 1024
STEP = 10
SEQS = 8
TOKENS = 8192


def draw_norm_vectors(key, part):
    key = jax.random.fold_in(key, 11)
    base = jax.random.truncated_normal(key, -3.0, 3.0, (4, D), jnp.float32)
    spread = jnp.array([0.1, 0.2, 0.2, 0.2], jnp.float32)[:, None]
    offset = jnp.array([1.0, 0.0, 0.0, 0.0], jnp.float32)[:, None]
    return base * spread + offset


def block_scale(stream_key, shape, split, low, top_value):
    factor_of, own = 1.0, jax.random.fold_in(stream_key, 6)
    for position, shards_of in split:
        steps = jnp.exp(jax.random.uniform(jax.random.fold_in(own, position), (shards_of,), jnp.float32, low / len(split), top_value / len(split)))
        factor_of = factor_of * jnp.repeat(steps, shape[position] // shards_of).reshape([-1 if axis == position else 1 for axis in range(len(shape))])
    return factor_of


def bell_draw(own_key, extent, deviation, limit, split=(), kind=jnp.bfloat16):
    values = jax.random.normal(own_key, extent, jnp.float32) * deviation
    if len(split) > 0:
        values = block_scale(own_key, extent, split, -0.22, 0.18) * values
    return jnp.clip(values, min=-limit, max=limit).astype(kind)


def setup_inputs(seed: int = 0) -> dict:
    streams_of = jax.random.split(jax.random.key(seed), 24)
    return {
        "inputs": bell_draw(streams_of[0], (TOKENS, D), 1.0, 6.0, ((0, 32),)),
        "cotangent": bell_draw(streams_of[1], (TOKENS, D), 1.0, 6.0, ((0, 32),)),
        "qkv_weight": bell_draw(streams_of[2], (D, 3, D), D ** -0.5, 0.125, ((0, 8), (2, 4)), jnp.float32),
        "qkv_first": bell_draw(streams_of[3], (D, 3, D), (0.11 * TOKENS ** 0.5), 64.0, ((0, 8), (2, 4)), jnp.float32),
        "qkv_second": jnp.clip(jnp.exp(math.log(32.768) - 1.3862944 * jax.random.uniform(streams_of[4], (D, 3, D), jnp.float32) ** block_scale(streams_of[4], (D, 3, D), ((0, 8), (2, 4)), -0.2, 0.2)), 8.192, 32.768),
        "dense_weight": bell_draw(streams_of[5], (D, D), (D * 64 // LENGTH) ** -0.5, 0.5, ((0, 8), (1, 4)), jnp.float32),
        "dense_first": bell_draw(streams_of[6], (D, D), (0.11 * (5 * TOKENS // LENGTH) ** 0.5), 4.0, ((0, 8), (1, 4)), jnp.float32),
        "dense_second": jnp.clip(jnp.exp(math.log(0.16) - 1.3862944 * jax.random.uniform(streams_of[7], (D, D), jnp.float32) ** block_scale(streams_of[7], (D, D), ((0, 8), (1, 4)), -0.2, 0.2)), 0.04, 0.16),
        "up_weight": bell_draw(streams_of[8], (D, FF), D ** -0.5, 0.125, ((0, 8), (1, 4)), jnp.float32),
        "up_first": bell_draw(streams_of[9], (D, FF), (0.033 * TOKENS ** 0.5), 16.0, ((0, 8), (1, 4)), jnp.float32),
        "up_second": jnp.clip(jnp.exp(math.log(2.94912) - 1.3862944 * jax.random.uniform(streams_of[10], (D, FF), jnp.float32) ** block_scale(streams_of[10], (D, FF), ((0, 8), (1, 4)), -0.2, 0.2)), 0.73728, 2.94912),
        "down_weight": bell_draw(streams_of[11], (D, FF), FF ** -0.5, 0.0625, ((0, 8), (1, 4)), jnp.float32),
        "down_first": bell_draw(streams_of[12], (D, FF), (0.066 * TOKENS ** 0.5), 32.0, ((0, 8), (1, 4)), jnp.float32),
        "down_second": jnp.clip(jnp.exp(math.log(11.79648) - 1.3862944 * jax.random.uniform(streams_of[13], (D, FF), jnp.float32) ** block_scale(streams_of[13], (D, FF), ((0, 8), (1, 4)), -0.2, 0.2)), 2.94912, 11.79648),
        "qkv_bias": bell_draw(streams_of[14], (3, D), 0.2, 1.25, ((1, 32),), jnp.float32),
        "qkv_bias_first": bell_draw(streams_of[15], (3, D), (0.11 * TOKENS ** 0.5), 64.0, ((1, 32),), jnp.float32),
        "qkv_bias_second": jnp.clip(jnp.exp(math.log(32.768) - 1.3862944 * jax.random.uniform(streams_of[16], (3, D), jnp.float32) ** block_scale(streams_of[16], (3, D), ((1, 32),), -0.2, 0.2)), 8.192, 32.768),
        "up_bias": bell_draw(streams_of[17], (FF,), 0.2, 1.25, ((0, 32),), jnp.float32),
        "up_bias_first": bell_draw(streams_of[18], (FF,), (0.033 * TOKENS ** 0.5), 16.0, ((0, 32),), jnp.float32),
        "up_bias_second": jnp.clip(jnp.exp(math.log(2.94912) - 1.3862944 * jax.random.uniform(streams_of[19], (FF,), jnp.float32) ** block_scale(streams_of[19], (FF,), ((0, 32),), -0.2, 0.2)), 0.73728, 2.94912),
        "norm_vectors": draw_norm_vectors(jax.random.fold_in(streams_of[23], 71), 0),
        "norm_first": bell_draw(streams_of[21], (4, D), (0.11 * TOKENS ** 0.5), 64.0, ((1, 8),), jnp.float32),
        "norm_second": jnp.clip(jnp.exp(math.log(32.768) - 1.3862944 * jax.random.uniform(streams_of[22], (4, D), jnp.float32) ** block_scale(streams_of[22], (4, D), ((1, 8),), -0.2, 0.2)), 8.192, 32.768),
    }


@jax.custom_vjp
def low(v):
    return lax.optimization_barrier(v.astype(jnp.bfloat16)).astype(jnp.float32)

@jax.custom_vjp
def low_back(v):
    return v

def low_keep(v):
    return (low(v), None)

def low_pass(kept, grad):
    return (grad,)

def back_keep(v):
    return (v, None)

def back_low(kept, grad):
    return (low(grad),)
low.defvjp(low_keep, low_pass)
low_back.defvjp(back_keep, back_low)
highest = lax.Precision.HIGHEST
norm_eps = 1e-05
beta_one = 0.9
beta_two = 0.999
epsilon = 1e-08
masked = -1e+30

def angles(positions):
    steps_half = jnp.arange(ROT // 2, dtype=jnp.float32)
    inverse = 1.0 / 10000.0 ** (steps_half * 2.0 / ROT)
    turned = positions[:, None] * inverse[None, :]
    return (jnp.cos(turned), jnp.sin(turned))

def rotate(field, cosine, sine):
    half = ROT // 2
    first = field[..., :half]
    second = field[..., half:ROT]
    cos_wide = cosine[:, None, :]
    sin_wide = sine[:, None, :]
    return jnp.concatenate([first * cos_wide - second * sin_wide, second * cos_wide + first * sin_wide, field[..., ROT:]], axis=-1)

def attend(query, keys, values):
    block = min(512, LENGTH)
    parts = query.reshape(LENGTH // block, block, HEADS, HEAD)
    starts = jnp.arange(LENGTH // block, dtype=jnp.int32) * block

    def one_block(items):
        part, start = items
        scores = jnp.einsum('bhe,lhe->hbl', part, keys, precision=highest, preferred_element_type=jnp.float32) * HEAD ** (-0.5)
        scores = low_back(scores)
        place = start + jnp.arange(block, dtype=jnp.int32)
        allowed = jnp.arange(LENGTH, dtype=jnp.int32)[None, :] <= place[:, None]
        scores = jnp.where(allowed[None], scores, masked)
        top = lax.optimization_barrier(jnp.max(scores, axis=2, keepdims=True))
        expo = jnp.exp(scores - top)
        probs = low(expo / lax.optimization_barrier(jnp.sum(expo, axis=2, keepdims=True)))
        return jnp.einsum('hbl,lhe->bhe', probs, values, precision=highest, preferred_element_type=jnp.float32)
    mixed = lax.map(jax.checkpoint(one_block), (parts, starts))
    return mixed.reshape(LENGTH, D)

def layer_rows(rows, params):
    qkv_low, dense_low, up_low, down_low, qkv_bias_low, up_bias_low, vectors_low = params
    centered = rows - lax.optimization_barrier(jnp.mean(rows, axis=1, keepdims=True))
    scale_inv = lax.rsqrt(lax.optimization_barrier(jnp.mean(centered * centered, axis=1, keepdims=True)) + norm_eps)
    normed = low(centered * scale_inv * vectors_low[0] + vectors_low[1])
    packed = low_back(jnp.einsum('td,dcf->tcf', normed, qkv_low, precision=highest, preferred_element_type=jnp.float32) + qkv_bias_low)
    cosine, sine = angles(jnp.arange(LENGTH, dtype=jnp.float32))
    query = low(rotate(packed[:, 0].reshape(LENGTH, HEADS, HEAD), cosine, sine))
    keys = low(rotate(packed[:, 1].reshape(LENGTH, HEADS, HEAD), cosine, sine))
    values = low(packed[:, 2].reshape(LENGTH, HEADS, HEAD))
    mixed = low(low_back(attend(query, keys, values)))
    attn_out = jnp.dot(mixed, dense_low.T, precision=highest, preferred_element_type=jnp.float32)
    hidden = low_back(jnp.dot(normed, up_low, precision=highest, preferred_element_type=jnp.float32) + up_bias_low)
    active = low(jax.nn.gelu(hidden, approximate=True))
    mlp_out = jnp.dot(active, down_low.T, precision=highest, preferred_element_type=jnp.float32)
    return rows + attn_out + mlp_out + vectors_low[2] + vectors_low[3]

def forward(source, qkv_weight, dense_weight, up_weight, down_weight, qkv_bias, up_bias, norm_vectors):
    params = tuple((low(member) for member in (qkv_weight, dense_weight, up_weight, down_weight, qkv_bias, up_bias, norm_vectors)))

    def step(carry, rows):
        return (carry, layer_rows(rows, params))
    _, result = lax.scan(jax.checkpoint(step), jnp.zeros((), jnp.float32), source.reshape(SEQS, LENGTH, D))
    return result.reshape(TOKENS, D)

def adam(weight, grad, first, second, rate, decay):
    first_new = beta_one * first + (1.0 - beta_one) * grad
    second_new = beta_two * second + (1.0 - beta_two) * grad * grad
    scaled_first = first_new / (1.0 - beta_one ** STEP)
    scaled_second = second_new / (1.0 - beta_two ** STEP)
    weight_new = weight - rate * (scaled_first / (jnp.sqrt(scaled_second) + epsilon) + decay * weight)
    return (weight_new, first_new, second_new)

def reference(inputs, cotangent, qkv_weight, qkv_first, qkv_second, dense_weight, dense_first, dense_second, up_weight, up_first, up_second, down_weight, down_first, down_second, qkv_bias, qkv_bias_first, qkv_bias_second, up_bias, up_bias_first, up_bias_second, norm_vectors, norm_first, norm_second):
    weights = (qkv_weight, dense_weight, up_weight, down_weight, qkv_bias, up_bias, norm_vectors)
    firsts = (qkv_first, dense_first, up_first, down_first, qkv_bias_first, up_bias_first, norm_first)
    seconds = (qkv_second, dense_second, up_second, down_second, qkv_bias_second, up_bias_second, norm_second)
    rates = (0.02, 0.02, 0.02, 0.02, 0.2, 0.2, 0.2)
    decays = (0.1, 0.1, 0.1, 0.1, 0.0, 0.0, 0.0)
    source = inputs.astype(jnp.float32)
    result, pullback = jax.vjp(forward, source, *weights)
    grads = pullback(cotangent.astype(jnp.float32))
    outs = [result.astype(jnp.bfloat16), grads[0]]
    for index in range(7):
        weight_new, first_new, second_new = adam(weights[index], grads[index + 1], firsts[index], seconds[index], rates[index], decays[index])
        outs += [grads[index + 1], weight_new, first_new, second_new]
    return tuple(outs)
```

```python
from functools import partial

import jax
import jax.numpy as jnp
import numpy as np
from jax import lax
from jax.experimental import pallas as pl
from jax.experimental.pallas import tpu as pltpu
from jax.sharding import Mesh
from jax.sharding import PartitionSpec as P

HEAD = 64
ROT = 32
LENGTH = 1024
STEP = 10
BLOCK = 256

norm_eps = 1e-05
beta_one = 0.9
beta_two = 0.999
epsilon = 1e-08
masked = -1e30
f32 = jnp.float32
bf16 = jnp.bfloat16


def ordered(index, own, other, axis):
    first = jnp.where(index == 0, own, other)
    second = jnp.where(index == 0, other, own)
    return jnp.concatenate([first, second], axis=axis)


def pick(value, index, axis):
    return lax.dynamic_index_in_dim(value, index, axis, keepdims=False)


MESH = pl.DeviceIdType.MESH


def here():
    return tuple(lax.axis_index(name) for name in ("z", "x", "y", "c"))


def remote(source, target, send, recv, device):
    return pltpu.make_async_remote_copy(
        src_ref=source,
        dst_ref=target,
        send_sem=send,
        recv_sem=recv,
        device_id=device,
        device_id_type=MESH,
    )


def span(start, size):
    return pl.ds(pl.multiple_of(start, 16), size)


class Tokens:
    def __init__(self, own, full, send, recv, local):
        self.own, self.full, self.send, self.recv, self.local = own, full, send, recv, local
        self.rows = own.shape[0]

    def at(self, x, y, c, part=None):
        start = ((x * 2 + y) * 2 + c) * self.rows
        cut = self.rows * 5 // 8
        if part is None:
            return self.full.at[span(start, self.rows)]
        return self.full.at[span(start + part * cut, self.rows - cut if part else cut)]

    def copy(self, index, arrives=False):
        _, x, y, c = here()
        to_x, to_y, to_c = {"x": 1 - x}, {"y": 1 - y}, {"c": 1 - c}
        owner, part, device, other = (
            ((x, y, c), None, to_x, (1 - x, y, c)),
            ((x, y, c), None, to_y, (x, 1 - y, c)),
            ((x, y, c), None, to_c, (x, y, 1 - c)),
            ((1 - x, y, c), 0, to_y, (1 - x, 1 - y, c)),
            ((1 - x, y, c), None, to_c, (1 - x, y, 1 - c)),
            ((x, 1 - y, c), 1, to_x, (1 - x, 1 - y, c)),
            ((x, 1 - y, c), None, to_c, (x, 1 - y, 1 - c)),
            ((1 - x, 1 - y, c), 0, to_c, (1 - x, 1 - y, 1 - c)),
            ((1 - x, 1 - y, c), 1, to_c, (1 - x, 1 - y, 1 - c)),
        )[index]
        target = self.at(*(other if arrives else owner), part)
        source = self.own if index < 3 else target
        return remote(source, target, self.send.at[index], self.recv.at[index], device)

    def own_copy(self):
        _, x, y, c = here()
        return pltpu.make_async_copy(self.own, self.at(x, y, c), self.local)

    def begin(self):
        self.own_copy().start()
        for index in range(3):
            self.copy(index).start()

    def middle(self):
        for first, index in ((0, 3), (1, 5)):
            self.copy(first, arrives=True).wait_recv()
            self.copy(index).start()
            self.copy(index + 1).start()

    def late(self):
        for first, index in ((3, 7), (5, 8)):
            self.copy(first, arrives=True).wait_recv()
            self.copy(index).start()

    def end(self):
        for index in (2, 4, 6, 7, 8):
            self.copy(index, arrives=True).wait_recv()
        for index in range(9):
            self.copy(index).wait_send()
        self.own_copy().wait()


class Line:
    def __init__(self, steps, halves, full, swap_sem, send, recv, local):
        self.steps, self.halves, self.full = steps, halves, full
        self.swap_sem, self.send, self.recv, self.local = swap_sem, send, recv, local
        self.rows = halves.shape[1]

    def at(self, z, x):
        return self.full.at[span((z * 2 + x) * self.rows, self.rows)]

    def own_copy(self):
        z, x, _, _ = here()
        return pltpu.make_async_copy(self.halves.at[x], self.at(z, x), self.local)

    def swap(self, arrives=False):
        z, x, _, _ = here()
        target = self.at(z, 1 - x if arrives else x)
        return remote(
            self.halves.at[1 - x], target, self.swap_sem.at[0], self.swap_sem.at[1], {"x": 1 - x}
        )

    def hop(self, step, which, way, arrives=False):
        z, x, _, _ = here()
        owner = z - step if way == 0 else z + step
        side = x if which == 0 else 1 - x
        device = {"z": jnp.clip(z + 1 if way == 0 else z - 1, 0, self.steps - 1)}
        owner = jnp.clip(owner, 0, self.steps - 1)
        target = self.at(owner, side)
        source = self.halves.at[x] if step == 0 and which == 0 else target
        index = (step - 1 if arrives else step) * 4 + which * 2 + way
        return remote(source, target, self.send.at[index], self.recv.at[index], device)

    def has(self, step, way):
        z = here()[0]
        return z >= step if way == 0 else z + step < self.steps

    def sends(self, step, way):
        z = here()[0]
        last = z < self.steps - 1 if way == 0 else z > 0
        return jnp.logical_and(self.has(step, way), last)

    def begin(self):
        self.own_copy().start()
        self.swap().start()
        self.push(0, 0)

    def push(self, step, which):
        if step < self.steps - 1:
            for way in (0, 1):

                @pl.when(self.sends(step, way))
                def _():
                    self.hop(step, which, way).start()

    def swapped(self):
        self.swap(arrives=True).wait_recv()
        self.push(0, 1)

    def turn(self, step, which):
        for way in (0, 1):

            @pl.when(self.has(step, way))
            def _():
                self.hop(step, which, way, arrives=True).wait_recv()

            if step < self.steps - 1:

                @pl.when(self.sends(step, way))
                def _():
                    self.hop(step, which, way).start()

    def end(self):
        self.own_copy().wait()
        self.swap().wait_send()
        for step in range(self.steps - 1):
            for which in (0, 1):
                for way in (0, 1):

                    @pl.when(self.sends(step, way))
                    def _():
                        self.hop(step, which, way).wait_send()


class SmallSum:
    def __init__(self, steps, mine, out, got, near_got, send, recv):
        self.steps, self.mine, self.out, self.got = steps, mine, out, got
        self.near_got, self.send, self.recv = near_got, send, recv

    def copy(self, k, arrives=False):
        z, x, _, _ = here()
        shards = self.steps * 2
        me = z * 2 + x
        other = lax.rem(me + k, shards)
        device = {"z": other // 2, "x": lax.rem(other, 2)}
        slot = other if arrives else me
        return remote(
            self.mine.at[other], self.got.at[slot], self.send.at[k], self.recv.at[slot], device
        )

    def each(self, act):
        def body(k, carry):
            act(k)
            return carry

        lax.fori_loop(1, self.steps * 2, body, 0)

    def begin(self):
        z, x, _, _ = here()
        self.each(lambda k: self.copy(k).start())
        self.got[z * 2 + x] = self.mine[z * 2 + x]

    def finish(self):
        _, _, y, c = here()
        shards = self.steps * 2
        self.each(lambda k: self.copy(k, arrives=True).wait_recv())
        total = self.got[0]
        for shard in range(1, shards):
            total = total + self.got[shard]
        self.out[...] = total
        half = total.shape[0] // 2
        at = y * 2 + c
        self.near_got[at] = total[:half]
        copies = []
        for index, (other_y, other_c) in enumerate(((y, 1 - c), (1 - y, c), (1 - y, 1 - c))):
            there = other_y * 2 + other_c
            sems = (self.send.at[shards + index], self.recv.at[shards + index])
            device = {"y": other_y, "c": other_c}
            leave = remote(self.near_got.at[at], self.near_got.at[at], *sems, device)
            leave.start()
            arrive = remote(self.near_got.at[there], self.near_got.at[there], *sems, device)
            copies.append((leave, arrive))
        for _, arrive in copies:
            arrive.wait_recv()
        near = self.near_got
        self.out[:half] = (near[0] + near[1]) + (near[2] + near[3])
        for leave, _ in copies:
            leave.wait_send()
        self.each(lambda k: self.copy(k).wait_send())


class SmallSizes:
    def __init__(self, norm, bias, up):
        self.norm, self.bias, self.up = norm, bias, up
        self.across = min(128, norm)
        self.norm_lines = norm // self.across


def put_lines(target, shard, row, line, start, size):
    wide = min(128, size)
    for index in range(size // wide):
        at = start + index * wide
        target[shard, row + index : row + index + 1, :wide] = line[:, at : at + wide]


def greet_wide(steps):
    z, x, y, c = here()
    shards = steps * 2
    barrier = pltpu.get_barrier_semaphore()

    def greet(k, carry):
        other = lax.rem(z * 2 + x + k, shards)
        device = {"z": other // 2, "x": lax.rem(other, 2)}
        pl.semaphore_signal(barrier, inc=1, device_id=device, device_id_type=MESH)
        return carry

    lax.fori_loop(1, shards, greet, 0)
    for device in ({"c": 1 - c}, {"y": 1 - y}, {"y": 1 - y, "c": 1 - c}):
        pl.semaphore_signal(barrier, inc=1, device_id=device, device_id_type=MESH)
    pl.semaphore_wait(barrier, shards + 2)


def rope_tables():
    steps_half = np.arange(ROT // 2, dtype=np.float32)
    inverse = np.float32(1.0) / np.float32(10000.0) ** (steps_half * np.float32(2.0 / ROT))
    turned = np.arange(LENGTH, dtype=np.float32)[:, None] * inverse[None, :].astype(np.float32)
    cosine, sine = (np.float32(part(turned.astype(np.float64))) for part in (np.cos, np.sin))
    none = np.zeros_like(sine)
    rest = np.zeros((LENGTH, HEAD - ROT), np.float32)
    keep = np.concatenate([cosine, cosine, rest + 1], axis=1)
    ahead = np.concatenate([-sine, none, rest], axis=1)
    behind = np.concatenate([none, sine, rest], axis=1)
    return np.stack([np.tile(table, (1, 2)).astype(np.float32) for table in (keep, ahead, behind)])


def gather_events(lines, steps):
    events = []
    for step in range(1, steps):
        for line in lines:
            for which in (0, 1):
                events.append(partial(line.turn, step, which))
    return events


def in_lanes(part, height):
    rows, across = part.shape
    if across < 128:
        part = jnp.concatenate([part, jnp.zeros((rows, 128 - across), f32)], axis=1)
    if rows < height:
        part = jnp.concatenate([part, jnp.zeros((height - rows, 128), f32)], axis=0)
    return part


class Sum:
    def __init__(self, steps, total, got, acc, leaving, kept, swapped, swap_sem, send, recv):
        self.steps, self.total, self.got, self.acc = steps, total, got, acc
        self.leaving, self.kept, self.swapped = leaving, kept, swapped
        self.swap_sem, self.send, self.recv = swap_sem, send, recv
        self.rows = leaving.shape[0]
        self.carried = False

    def part(self, owner, which):
        x = here()[1]
        side = 1 - x if which == 0 else x
        owner = jnp.clip(owner, 0, self.steps - 1)
        return span((owner * 2 + side) * self.rows, self.rows)

    def slot(self, step, which, way):
        index = step - 1 if way == 0 else self.steps + 1 - step
        return self.got.at[index, pl.ds(which * self.rows, self.rows)]

    def hop(self, step, which, way, source):
        z = here()[0]
        device = {"z": jnp.clip(z - 1 if way == 0 else z + 1, 0, self.steps - 1)}
        index = (step - 1) * 4 + which * 2 + way
        target = self.slot(step, which, way)
        source = target if source is None else source
        return remote(source, target, self.send.at[index], self.recv.at[index], device)

    def owner(self, step, way):
        z = here()[0]
        return z - step if way == 0 else z + step

    def sends(self, step, way):
        owner = self.owner(step, way)
        return owner >= 0 if way == 0 else owner < self.steps

    def inner(self, way):
        z = here()[0]
        return z < self.steps - 1 if way == 0 else z > 0

    def turn(self, step, which):
        for way in (0, 1):
            rows = self.part(self.owner(step, way), which)
            if step == self.steps - 1:

                @pl.when(self.sends(step, way))
                def _():
                    self.hop(step, which, way, self.total.at[rows]).start()

            else:

                @pl.when(jnp.logical_and(self.sends(step, way), self.inner(way)))
                def _():
                    if not (self.carried and step == self.steps - 2):
                        self.hop(step + 1, which, way, None).wait_recv()
                    here_now = self.slot(step + 1, which, way)
                    here_now[...] = (
                        here_now[...].astype(f32) + self.total[rows, :].astype(f32)
                    ).astype(bf16)
                    self.hop(step, which, way, here_now).start()

                @pl.when(jnp.logical_and(self.sends(step, way), jnp.logical_not(self.inner(way))))
                def _():
                    self.hop(step, which, way, self.total.at[rows]).start()

    def swap(self):
        x = here()[1]
        return remote(
            self.leaving, self.swapped, self.swap_sem.at[0], self.swap_sem.at[1], {"x": 1 - x}
        )

    def final(self, which):
        z = here()[0]
        self.acc[...] = self.total[self.part(z, which), :].astype(f32)
        for way in (0, 1):

            @pl.when(self.inner(way))
            def _():
                self.hop(1, which, way, None).wait_recv()
                self.acc[...] += self.slot(1, which, way)[...].astype(f32)

        if which == 0:
            self.leaving[...] = self.acc[...].astype(bf16)
            self.swap().start()
        elif self.kept is not None:
            self.kept[...] = self.acc[...]

    def begin(self):
        for which in (0, 1):
            self.turn(self.steps - 1, which)

    def events(self):
        out = []
        for step in range(self.steps - 2, 0, -1):
            out += [partial(self.turn, step, which) for which in (0, 1)]
        return out + [partial(self.final, which) for which in (0, 1)]

    def end(self):
        self.swap().wait_recv()
        self.swap().wait_send()
        for step in range(self.steps - 1 - self.carried, 0, -1):
            for which in (0, 1):
                for way in (0, 1):

                    @pl.when(self.sends(step, way))
                    def _():
                        self.hop(step, which, way, None).wait_send()


class FirstHop(Sum):
    def __init__(self, steps, total, got, rows, send, recv):
        self.steps, self.total, self.got, self.rows = steps, total, got, rows
        self.send, self.recv = send, recv

    def slot(self, step, which, way):
        return self.got.at[way, pl.ds(which * self.rows, self.rows)]

    def end(self):
        z = here()[0]
        last = self.steps - 1
        for way, place in ((0, last - 1), (1, 1)):
            for which in (0, 1):

                @pl.when(z == place)
                def _():
                    self.hop(last, which, way, None).wait_recv()

                @pl.when(self.sends(last, way))
                def _():
                    self.hop(last, which, way, None).wait_send()


class SumPair:
    def __init__(self, *members):
        self.members = members

    def begin(self):
        for member in self.members:
            member.begin()

    def events(self):
        def together(parts):
            for part in parts:
                part()

        return [partial(together, parts) for parts in zip(*(m.events() for m in self.members))]

    def end(self):
        for member in self.members:
            member.end()


def merged(*lists):
    keyed = []
    for number, entries in enumerate(lists):
        for index, entry in enumerate(entries):
            keyed.append(((index + 1) / (len(entries) + 1), number, index, entry))
    return [entry[3] for entry in sorted(keyed, key=lambda item: item[:3])]


def work_loop(count, tile, events):
    def body(index, carry):
        tile(index)
        for turn, due in events.items():

            @pl.when(index == turn)
            def _(due=due):
                for event in due:
                    event()

        return carry

    lax.fori_loop(0, count, body, 0)


def one_each(events):
    return {index: [event] for index, event in enumerate(events)}


def dot(a, b, dims):
    return lax.dot_general(a, b, (dims, ((), ())), preferred_element_type=f32)


TILE = 256


def turned(index, model, rows):
    z = here()[0]
    first = (1 - jnp.minimum(z, 1)) * ((model - 2 * rows) // TILE)
    return lax.rem(index + first, model // TILE)


def tile_of(index):
    return pl.ds(pl.multiple_of(index * TILE, TILE), TILE)


def front_kernel(
    steps,
    small_sizes,
    norm_ref,
    qkv_bias_ref,
    up_own_ref,
    inputs_hbm,
    cot_ref,
    tables_hbm,
    qkv_hbm,
    dense_hbm,
    up_hbm,
    down_hbm,
    vectors_ref,
    attn_out,
    grad_out,
    normed_out,
    cot_out,
    qkv_out,
    dense_out,
    up_out,
    down_full,
    active_out,
    slope_out,
    down_part,
    carry,
    qkv_kept,
    qkv_swapped,
    dense_kept,
    dense_swapped,
    small_ref,
    small_all,
    normed_all,
    cot_all,
    qkv_full,
    dense_full,
    up_full,
    active,
    slope,
    normed,
    qkv_ref,
    dense_ref,
    wide_ref,
    bias_ref,
    bias_up_ref,
    packed_ref,
    g_ref,
    dk_ref,
    dv_ref,
    qkv_got,
    dense_got,
    tables,
    token_send,
    token_recv,
    small_send,
    small_recv,
    swap_sem,
    line_send,
    line_recv,
    sum_swap,
    sum_send,
    sum_recv,
    local,
    load,
    store,
    slope_store,
):
    seq, pair = pl.program_id(0), pl.program_id(1)
    turn_now = seq * pl.num_programs(1) + pair
    z, x, y, c = here()
    shards = steps * 2
    me = z * 2 + x
    depth, width = dense_ref.shape[1:]
    wide = 3 * width
    tokens, model = normed_all.shape
    hidden = up_full.shape[1]
    up_line, qkv_line, dense_line, down_line = (
        Line(
            steps,
            halves,
            full,
            swap_sem.at[index],
            line_send.at[index],
            line_recv.at[index],
            local.at[index],
        )
        for index, (halves, full) in enumerate(
            (
                (wide_ref.at[0], up_full),
                (qkv_ref, qkv_full),
                (dense_ref, dense_full),
                (wide_ref.at[1], down_full),
            )
        )
    )
    lines = [qkv_line, dense_line]
    cots = Tokens(cot_ref, cot_all, token_send.at[0], token_recv.at[0], local.at[4])
    units = Tokens(normed, normed_all, token_send.at[1], token_recv.at[1], local.at[5])
    cuts = (slice(0, wide), slice(wide, wide + width))
    qkv_sum, dense_sum = (
        Sum(
            steps,
            terms,
            got,
            slope.at[0, pl.ds(0, depth), cut],
            wide_ref.at[0, 0, :, cut],
            None,
            swapped,
            sum_swap.at[index],
            sum_send.at[index],
            sum_recv.at[index],
        )
        for index, (terms, got, cut, swapped) in enumerate(
            (
                (qkv_full, qkv_got, cuts[0], qkv_swapped),
                (dense_full, dense_got, cuts[1], dense_swapped),
            )
        )
    )
    narrow = SumPair(qkv_sum, dense_sum)
    first_hop = FirstHop(steps, up_full, carry, depth, sum_send.at[2], sum_recv.at[2])

    def copy_in(index, source, target):
        return pltpu.make_async_copy(source, target, load.at[index])

    narrow_loads = [
        copy_in(kind, qkv_hbm.at[kind], packed_ref.at[pl.ds(kind * depth, depth), 0 : 2 * width])
        for kind in range(3)
    ]
    narrow_loads.append(
        copy_in(3, dense_hbm, packed_ref.at[pl.ds(3 * depth, depth), 0 : 2 * width])
    )

    def wide_loads(index, source):
        return [
            copy_in(
                4 + index * 2 + half,
                source.at[:, half * hidden : (half + 1) * hidden],
                slope.at[half, pl.ds(0, depth)],
            )
            for half in (0, 1)
        ]

    up_loads, down_loads = wide_loads(0, up_hbm), wide_loads(1, down_hbm)

    def copy_out(index, source, target):
        return pltpu.make_async_copy(source, target, store.at[index])

    stores = {
        "cot": copy_out(0, cot_all, cot_out),
        "normed": copy_out(1, normed_all, normed_out),
        "up": copy_out(2, up_full, up_out),
        "active": copy_out(3, active, active_out),
        "qkv": copy_out(4, qkv_full, qkv_out),
        "dense": copy_out(5, dense_full, dense_out),
        "grad": copy_out(6, active.at[:, 0:wide], grad_out),
        "attn": copy_out(7, active.at[:, wide : wide + width], attn_out),
        "down_part": copy_out(8, up_full, down_part),
        "qkv_kept": copy_out(9, slope.at[0, pl.ds(0, depth), cuts[0]], qkv_kept),
        "dense_kept": copy_out(10, slope.at[0, pl.ds(0, depth), cuts[1]], dense_kept),
    }

    def peer(k):
        other = lax.rem(me + k, shards)
        return other, {"z": other // 2, "x": lax.rem(other, 2)}

    def small_copy(k, arrives=False):
        other, device = peer(k)
        slot = other if arrives else me
        return remote(
            small_ref,
            small_all.at[slot],
            small_send.at[k],
            small_recv.at[slot],
            device,
        )

    def each_peer(act):
        def body(k, carry):
            act(k)
            return carry

        lax.fori_loop(1, shards, body, 0)

    def piece(shard, row, size):
        block = small_all[shard].astype(f32)
        across = min(128, size)
        return [block[row + k : row + k + 1, :across] for k in range(size // across)]

    def lower_wide(index, loads):
        for copy in loads:
            copy.wait()
        for half in (0, 1):
            wide_ref[index, half] = slope[half, :depth, :].astype(bf16)

    def gather_all():
        own_loads = [copy_in(8, inputs_hbm, normed), copy_in(9, tables_hbm, tables)]
        for copy in up_loads + narrow_loads + own_loads:
            copy.start()
        barrier = pltpu.get_barrier_semaphore()
        each_peer(
            lambda k: pl.semaphore_signal(
                barrier, inc=1, device_id=peer(k)[1], device_id_type=MESH
            )
        )
        for device in ({"y": 1 - y}, {"c": 1 - c}):
            pl.semaphore_signal(barrier, inc=1, device_id=device, device_id_type=MESH)
        lines_norm = [
            norm_ref[row : row + 1, cut * small_sizes.across : (cut + 1) * small_sizes.across]
            for row in range(4)
            for cut in range(small_sizes.norm_lines)
        ]
        parts = [in_lanes(jnp.concatenate(lines_norm, axis=0), 8)]
        parts += [in_lanes(qkv_bias_ref[...], 3), in_lanes(up_own_ref[...], 5)]
        small_ref[...] = jnp.concatenate(parts, axis=0).astype(bf16)
        for copy in narrow_loads:
            copy.wait()
        for half in (0, 1):
            cut = slice(half * width, (half + 1) * width)
            for kind in range(3):
                at = slice(kind * width, (kind + 1) * width)
                rows = slice(kind * depth, (kind + 1) * depth)
                qkv_ref[half, :, at] = packed_ref[rows, cut].astype(bf16)
            dense_ref[half] = packed_ref[3 * depth : 4 * depth, cut].astype(bf16)
        pl.semaphore_wait(barrier, shards + 1)
        for line in lines:
            line.begin()
        each_peer(lambda k: small_copy(k).start())
        small_all[me] = small_ref[...]
        cots.begin()
        each_peer(lambda k: small_copy(k, arrives=True).wait_recv())
        for row in range(4):
            parts = []
            for shard in range(shards):
                parts += piece(shard, row * small_sizes.norm_lines, small_sizes.norm)
            vectors_ref[row : row + 1, :] = jnp.concatenate(parts, axis=1)
        gain, shift = vectors_ref[0:1, :], vectors_ref[1:2, :]
        chunk = 32

        for copy in own_loads:
            copy.wait()

        def norm(index, carry):
            rows = span(index * chunk, chunk)
            source = normed[rows, :].astype(f32)
            centered = source - jnp.mean(source, axis=1, keepdims=True)
            scale = lax.rsqrt(jnp.mean(centered * centered, axis=1, keepdims=True) + norm_eps)
            normed[rows, :] = (centered * scale * gain + shift).astype(bf16)
            return carry

        lax.fori_loop(0, normed.shape[0] // chunk, norm, 0)
        units.begin()
        for line in lines:
            line.swapped()
        lower_wide(0, up_loads)
        for copy in down_loads:
            copy.start()
        parts = []
        for kind in range(3):
            for part in range(steps):
                parts += piece(x * steps + part, 8 + kind, small_sizes.bias)
        bias_ref[...] = jnp.concatenate(parts, axis=1)
        parts = []
        for part in range(steps):
            parts += piece(x * steps + part, 11, small_sizes.up)
        bias_up_ref[...] = jnp.concatenate(parts, axis=1)
        lower_wide(1, down_loads)
        for step in range(1, steps):
            for line in lines:
                for which in (0, 1):
                    line.turn(step, which)
            if step == max(steps - 2, 1):
                up_line.begin()
                cots.middle()
                units.middle()
        cots.late()
        units.late()
        cots.end()
        units.end()
        for line in lines:
            line.end()
        for name in ("cot", "normed", "qkv", "dense"):
            stores[name].start()
        each_peer(lambda k: small_copy(k).wait_send())
        up_line.swapped()

    def slope_copy(index):
        slot = lax.rem(index, 2)
        return pltpu.make_async_copy(
            slope.at[slot], slope_out.at[tile_of(index), :], slope_store.at[slot]
        )

    def hidden_tile(index):
        at = tile_of(index)
        before = dot(normed_all[at, :], up_full[...], ((1,), (0,))) + bias_up_ref[...]
        inner = (2.0 / 3.141592653589793) ** 0.5
        square = before * before
        bent = jnp.tanh(inner * (before + 0.044715 * (square * before)))
        gate = 0.5 * (1.0 + bent)
        active[at, :] = (before * gate).astype(bf16)

        @pl.when(index >= 2)
        def _():
            slope_copy(index - 2).wait()

        slope[lax.rem(index, 2)] = gate + 0.5 * before * (1.0 - bent * bent) * (
            inner * (1.0 + 3.0 * 0.044715 * square)
        )
        slope_copy(index).start()

    def down_tile(index):
        at = tile_of(index)
        up_full[at, :] = dot(cot_all[:, at], active[...], ((0,), (0,))).astype(bf16)

    up_hops, down_hops = gather_events([up_line], steps), gather_events([down_line], steps)
    sums = narrow.events()

    def up_and_down():
        up_hops[3]()
        down_line.begin()

    when = {(0, 0): up_hops[0], (0, 2): up_hops[1], (1, 2): up_hops[2], (2, 1): up_and_down}

    def check(now, point):
        if (now, point) in when:
            pl.when(turn_now == now)(when[(now, point)])

    def dense_tile(index):
        at = tile_of(index)
        dense_full[at, :] = dot(
            cot_all[:, at], active[:, wide : wide + width], ((0,), (0,))
        ).astype(bf16)

    def qkv_tile(index):
        at = tile_of(turned(index, model, depth))
        qkv_full[at, :] = dot(normed_all[:, at], active[:, :wide], ((0,), (0,))).astype(bf16)

    def finish():
        for name in ("grad", "attn"):
            stores[name].start()
        for name in ("qkv", "dense"):
            stores[name].wait()
        work_loop(model // TILE, dense_tile, {})
        dense_sum.begin()
        work_loop(model // TILE, qkv_tile, {1: [qkv_sum.begin]})
        for event in up_hops[4:]:
            event()
        up_line.end()
        stores["up"].start()
        down_line.swapped()
        for name in ("grad", "attn"):
            stores[name].wait()
        count = tokens // TILE
        work_loop(count, hidden_tile, {2: down_hops[:1], 5: sums[:1]})
        stores["active"].start()
        stores["up"].wait()
        work_loop(model // TILE, down_tile, {1: down_hops[1:2], 4: sums[1:2]})
        stores["down_part"].start()
        slope_copy(count - 2).wait()
        slope_copy(count - 1).wait()
        for event in merged(down_hops[2:-2], sums[2:-2]) + [first_hop.begin] + sums[-2:]:
            event()
        for name in ("qkv_kept", "dense_kept"):
            stores[name].start()
        for event in down_hops[-2:]:
            event()
        down_line.end()
        first_hop.end()
        narrow.end()
        for name in ("cot", "normed", "active", "down_part", "qkv_kept", "dense_kept"):
            stores[name].wait()

    @pl.when(turn_now == 0)
    def _():
        gather_all()

    @pl.when(pair == 0)
    def _():
        def products(index):
            rows, at = tile_of(seq * (LENGTH // TILE) + index), tile_of(index)
            packed_ref[at, :] = dot(normed_all[rows, :], qkv_full[...], ((1,), (0,))) + bias_ref[...]
            g_ref[at, :] = dot(cot_all[rows, :], dense_full[...], ((1,), (0,))).astype(bf16)

        work_loop(LENGTH // TILE, products, {})

    for now in range(4):
        check(now, 0)
    keep, ahead, behind = (tables[index] for index in range(3))
    half = ROT // 2

    def turn(field, sign):
        up = pltpu.roll(field, field.shape[1] - half, 1)
        down = pltpu.roll(field, half, 1)
        return field * keep + sign * (up * ahead + down * behind)

    def lanes_of(kind):
        return pl.ds(pl.multiple_of(kind * width + pair * 2 * HEAD, 2 * HEAD), 2 * HEAD)

    factor = HEAD ** (-0.5)
    query = turn(packed_ref[:, lanes_of(0)], 1.0).astype(bf16) * jnp.asarray(factor, bf16)
    keys = turn(packed_ref[:, lanes_of(1)], 1.0).astype(bf16)
    values = packed_ref[:, lanes_of(2)].astype(bf16)
    grads = g_ref[:, lanes_of(0)]
    inside = lax.broadcasted_iota(jnp.int32, (BLOCK, BLOCK), 1) <= lax.broadcasted_iota(
        jnp.int32, (BLOCK, BLOCK), 0
    )

    mixed_all, dq_all, dk_all, dv_all = [], [], [], []
    for head in range(2):
        lanes = slice(head * HEAD, (head + 1) * HEAD)
        qh, kh, vh, gh = query[:, lanes], keys[:, lanes], values[:, lanes], grads[:, lanes]
        mixed_rows, dq_rows = [], []
        dk_ref[...] = jnp.zeros_like(dk_ref)
        dv_ref[...] = jnp.zeros_like(dv_ref)
        for block in range(LENGTH // BLOCK):
            rows = slice(block * BLOCK, (block + 1) * BLOCK)
            seen = (block + 1) * BLOCK
            q, g, k, v = qh[rows], gh[rows], kh[:seen], vh[:seen]
            scores = dot(q, k, ((1,), (1,)))
            last = jnp.where(inside, scores[:, block * BLOCK :], masked)
            if block > 0:
                scores = jnp.concatenate([scores[:, : block * BLOCK], last], axis=1)
            else:
                scores = last
            top = jnp.max(scores, axis=1, keepdims=True)
            expo = jnp.exp(scores - top)
            probs = expo * (1.0 / jnp.sum(expo, axis=1, keepdims=True))
            low = probs.astype(bf16)
            mixed_rows.append(dot(low, v, ((1,), (0,))))
            grad_probs = dot(g, v, ((1,), (1,)))
            inner = jnp.sum(probs * grad_probs, axis=1, keepdims=True)
            grad_scores = (probs * (grad_probs - inner)).astype(bf16)
            dq_rows.append(dot(grad_scores, k, ((1,), (0,))) * factor)
            dk_ref[:seen] += dot(grad_scores, q, ((0,), (0,)))
            dv_ref[:seen] += dot(low, g, ((0,), (0,)))
        mixed_all.append(jnp.concatenate(mixed_rows, axis=0))
        dq_all.append(jnp.concatenate(dq_rows, axis=0))
        dk_all.append(dk_ref[...])
        dv_all.append(dv_ref[...])
        if head == 0:
            for now in range(4):
                check(now, 1)
    mixed = jnp.concatenate(mixed_all, axis=1)
    gq = turn(jnp.concatenate(dq_all, axis=1), -1.0)
    gk = turn(jnp.concatenate(dk_all, axis=1), -1.0)
    gv = jnp.concatenate(dv_all, axis=1)
    rows = pl.ds(pl.multiple_of(seq * LENGTH, LENGTH), LENGTH)
    for kind, part in enumerate((gq, gk, gv, mixed)):
        active[rows, lanes_of(kind)] = part.astype(bf16)

    for now in range(4):
        check(now, 2)

    pl.when(turn_now == 3)(finish)


def front(norm, qkv_bias, up_bias, inputs, cotangent, tables, qkv, dense, up, down, sizes, steps):
    shards = steps * 2
    rows, model = inputs.shape
    tokens = 8 * rows
    depth, width = dense.shape
    width = width // 2
    wide = 3 * width
    hidden = up.shape[1] // 2
    pairs = width // (2 * HEAD)
    seqs = tokens // LENGTH
    assert seqs * pairs == 4 and wide + width <= hidden and 4 * depth <= LENGTH
    whole = pl.BlockSpec(memory_space=pltpu.VMEM)
    anywhere = pl.BlockSpec(memory_space=pl.ANY)
    dma = pltpu.SemaphoreType.DMA
    hops = max(steps - 1, 1) * 4
    low = {
        name: jax.ShapeDtypeStruct(shape, bf16)
        for name, shape in (
            ("tokens", (tokens, model)),
            ("attn", (tokens, width)),
            ("grad", (tokens, wide)),
            ("hidden", (tokens, hidden)),
            ("qkv", (model, wide)),
            ("dense", (model, width)),
            ("up", (model, hidden)),
        )
    }
    flops = seqs * pairs * 2 * 7 * 2 * LENGTH * LENGTH * HEAD
    flops += 4 * tokens * model * (wide + width + hidden)
    return pl.pallas_call(
        partial(front_kernel, steps, sizes),
        grid=(seqs, pairs),
        in_specs=[whole] * 3 + [anywhere] * 7,
        out_specs=[whole] + [anywhere] * 16,
        out_shape=[
            jax.ShapeDtypeStruct((4, model), f32),
            low["attn"],
            low["grad"],
            low["tokens"],
            low["tokens"],
            low["qkv"],
            low["dense"],
            low["up"],
            low["up"],
            low["hidden"],
            jax.ShapeDtypeStruct((tokens, hidden), f32),
            low["up"],
            jax.ShapeDtypeStruct((2, 2 * depth, hidden), bf16),
            jax.ShapeDtypeStruct((depth, wide), f32),
            jax.ShapeDtypeStruct((depth, wide), bf16),
            jax.ShapeDtypeStruct((depth, width), f32),
            jax.ShapeDtypeStruct((depth, width), bf16),
        ],
        scratch_shapes=[
            pltpu.VMEM((16, 128), bf16),
            pltpu.VMEM((shards, 16, 128), bf16),
            pltpu.VMEM((tokens, model), bf16),
            pltpu.VMEM((tokens, model), bf16),
            pltpu.VMEM((model, wide), bf16),
            pltpu.VMEM((model, width), bf16),
            pltpu.VMEM((model, hidden), bf16),
            pltpu.VMEM((tokens, hidden), bf16),
            pltpu.VMEM((2, TILE, hidden), f32),
            pltpu.VMEM((rows, model), bf16),
            pltpu.VMEM((2, depth, wide), bf16),
            pltpu.VMEM((2, depth, width), bf16),
            pltpu.VMEM((2, 2, depth, hidden), bf16),
            pltpu.VMEM((1, wide), f32),
            pltpu.VMEM((1, hidden), f32),
            pltpu.VMEM((LENGTH, wide), f32),
            pltpu.VMEM((LENGTH, width), bf16),
            pltpu.VMEM((LENGTH, HEAD), f32),
            pltpu.VMEM((LENGTH, HEAD), f32),
            pltpu.VMEM((steps + 1, 2 * depth, wide), bf16),
            pltpu.VMEM((steps + 1, 2 * depth, width), bf16),
            pltpu.VMEM(tables.shape, f32),
            dma((2, 9)),
            dma((2, 9)),
            dma((shards,)),
            dma((shards,)),
            dma((4, 2)),
            dma((4, hops)),
            dma((4, hops)),
            dma((2, 2)),
            dma((3, hops)),
            dma((3, hops)),
            dma((6,)),
            dma((10,)),
            dma((11,)),
            dma((2,)),
        ],
        cost_estimate=pl.CostEstimate(
            flops=flops, bytes_accessed=2**27, transcendentals=seqs * pairs * 2**21
        ),
        compiler_params=pltpu.CompilerParams(
            collective_id=0, has_side_effects=True, vmem_limit_bytes=63 * 2**20
        ),
    )(norm, qkv_bias, up_bias, inputs, cotangent, tables, qkv, dense, up, down)


class TokenSum:
    def __init__(self, product, away, near, one, two, last, out, send, recv):
        self.product, self.away, self.near = product, away, near
        self.one, self.two, self.last, self.out = one, two, last, out
        self.send, self.recv = send, recv
        self.half = out.shape[1] // 2
        self.width = out.shape[2]

    def copy(self, source, target, index, device):
        return remote(source, target, self.send.at[index], self.recv.at[index], device)

    def to_core(self, k):
        c = here()[3]
        return self.copy(self.away.at[k], self.near.at[k], k, {"c": 1 - c})

    def rows(self, which):
        return pl.ds(which * self.half, self.half)

    def first(self, xx, yy):
        x = here()[1]
        source = self.near.at[xx * 2 + yy, self.rows(0)]
        return self.copy(source, self.one.at[yy], 4 + yy, {"x": 1 - x})

    def second(self, xx, yy):
        y = here()[2]
        source = self.near.at[xx * 2 + yy, self.rows(1)]
        return self.copy(source, self.two.at[xx], 6 + xx, {"y": 1 - y})

    def third(self, which):
        _, x, y, _ = here()
        source = self.one.at[1 - y] if which == 0 else self.two.at[1 - x]
        device = {"y": 1 - y} if which == 0 else {"x": 1 - x}
        return self.copy(source, self.last.at[which], 8 + which, device)

    def columns(self):
        size = self.width // 2
        return [slice(index * size, (index + 1) * size) for index in range(4)]

    def give(self, k):
        c = here()[3]
        for cut in self.columns():
            self.away[k, :, cut] = self.product(k * 2 + 1 - c, cut).astype(bf16)
        self.to_core(k).start()

    def take(self, j):
        _, x, y, c = here()
        xx, yy = lax.rem(x + 1 - j // 2, 2), lax.rem(y + 1 - lax.rem(j, 2), 2)
        k = xx * 2 + yy
        self.to_core(k).wait_recv()
        for cut in self.columns():
            term = self.product(k * 2 + c, cut)
            self.near[k, :, cut] = (self.near[k, :, cut].astype(f32) + term).astype(bf16)

        @pl.when(j < 2)
        def _():
            self.first(xx, yy).start()

        @pl.when(lax.rem(j, 2) == 0)
        def _():
            self.second(xx, yy).start()

    def middle(self):
        _, x, y, _ = here()
        self.first(x, 1 - y).wait_recv()
        block = self.one.at[1 - y]
        block[...] = (
            block[...].astype(f32) + self.near[x * 2 + 1 - y, self.rows(0)].astype(f32)
        ).astype(bf16)
        self.third(0).start()
        self.second(1 - x, y).wait_recv()
        block = self.two.at[1 - x]
        block[...] = (
            block[...].astype(f32) + self.near[(1 - x) * 2 + y, self.rows(1)].astype(f32)
        ).astype(bf16)
        self.third(1).start()

    def final(self):
        _, x, y, _ = here()
        self.first(x, y).wait_recv()
        self.second(x, y).wait_recv()
        for which, got in ((0, self.one.at[y]), (1, self.two.at[x])):
            self.third(which).wait_recv()
            for side in (0, 1):
                cut = slice(side * self.width, (side + 1) * self.width)
                self.out[side, self.rows(which), :] = (
                    self.near[x * 2 + y, self.rows(which), cut].astype(f32)
                    + got[:, cut].astype(f32)
                    + self.last[which, :, cut].astype(f32)
                )

    def end_core(self):
        for k in range(4):
            self.to_core(k).wait_send()

    def end(self):
        _, x, y, _ = here()
        for yy in range(2):
            self.first(1 - x, yy).wait_send()
        for xx in range(2):
            self.second(xx, 1 - y).wait_send()
        for which in (0, 1):
            self.third(which).wait_send()


def back_kernel(
    steps,
    small,
    part_hbm,
    carry,
    cot_hbm,
    down_hbm,
    slope_hbm,
    attn_hbm,
    active_hbm,
    dense_hbm,
    normed_hbm,
    grad_packed_hbm,
    qkv_hbm,
    up_hbm,
    inputs_hbm,
    cot_own_hbm,
    vectors_ref,
    down_kept,
    down_swapped,
    up_kept,
    up_swapped,
    output_ref,
    input_grad,
    small_ref,
    rows_all,
    weight,
    slope,
    grad,
    attn,
    active,
    dense,
    away,
    near,
    one,
    two,
    last,
    token_send,
    token_recv,
    free,
    total,
    down_got,
    up_got,
    acc,
    leaving,
    swap_sem,
    sum_send,
    sum_recv,
    load,
    fetch,
    vector_sums,
    small_mine,
    small_got,
    near_got,
    small_send,
    small_recv,
):
    z, x, y, c = here()
    loads = [
        pltpu.make_async_copy(source, target, load.at[index])
        for index, (source, target) in enumerate(
            (
                (part_hbm, total),
                (cot_hbm, rows_all),
                (down_hbm, weight),
                (attn_hbm, attn),
                (active_hbm, active),
                (dense_hbm, dense),
            )
        )
    ]
    for copy in loads[:1] + loads[2:] + loads[1:2]:
        copy.start()
    carried = [
        (z == place, pltpu.make_async_copy(carry.at[way], down_got.at[slot], load.at[8]))
        for way, place, slot in ((0, steps - 2, steps - 2), (1, 1, 2))
    ]
    for here_now, copy in carried:
        pl.when(here_now)(copy.start)
    greet_wide(steps)

    def slope_copy(index):
        slot = lax.rem(index, 2)
        return pltpu.make_async_copy(
            slope_hbm.at[tile_of(index), :], slope.at[slot], fetch.at[slot]
        )

    slope_copy(0).start()
    tokens, model = cot_hbm.shape
    count = tokens // TILE
    down_sum, up_sum = (
        Sum(
            steps,
            terms,
            got,
            acc,
            leaving,
            None,
            swapped,
            swap_sem.at[index],
            sum_send.at[index],
            sum_recv.at[index],
        )
        for index, (terms, got, swapped) in enumerate(
            ((total, down_got, down_swapped), (active, up_got, up_swapped))
        )
    )
    keeps = [
        pltpu.make_async_copy(acc, kept, load.at[index + 6])
        for index, kept in enumerate((down_kept, up_kept))
    ]

    def out_product(tile, cut):
        at = tile_of(tile)
        return dot(attn[at, :], dense[cut, :], ((1,), (1,))) + dot(
            active[at, :], weight[cut, :], ((1,), (1,))
        )

    wide = grad_packed_hbm.shape[1]

    def normed_product(tile, cut):
        at = tile_of(tile)
        return dot(rows_all[at, :wide], rows_all[cut, wide : 2 * wide], ((1,), (1,))) + dot(
            grad[at, :], weight[cut, :], ((1,), (1,))
        )

    buffers = (away, near, one, two, last, slope)
    out_tokens, normed_tokens = (
        TokenSum(product, *buffers, token_send.at[index], token_recv.at[index])
        for index, product in enumerate((out_product, normed_product))
    )
    down_sum.carried = True
    loads[0].wait()
    for here_now, copy in carried:
        pl.when(here_now)(copy.wait)
    events = down_sum.events()
    for event in events[:2]:
        event()
    for copy in loads[2:]:
        copy.wait()
    work_loop(4, out_tokens.give, {})
    work_loop(4, out_tokens.take, {3: events[2:3]})
    out_tokens.end_core()
    inputs_load = pltpu.make_async_copy(inputs_hbm, away.at[0], load.at[0])
    cot_load = pltpu.make_async_copy(cot_own_hbm, away.at[1], load.at[1])
    inputs_load.start()
    loads[1].wait()

    def grad_tile(index, bias_sum):
        at = tile_of(index)

        @pl.when(index + 1 < count)
        def _():
            slope_copy(index + 1).start()

        slope_copy(index).wait()
        term = dot(rows_all[at, :], weight[...], ((1,), (0,))) * slope[lax.rem(index, 2)]
        low = term.astype(bf16)
        grad[at, :] = low

        @pl.when(index == 4)
        def _():
            for event in events[3:-2]:
                event()

        return bias_sum + jnp.sum(low.astype(f32), axis=0, keepdims=True)

    hidden_sum = lax.fori_loop(0, count, grad_tile, jnp.zeros((1, slope.shape[2]), f32))
    normed_load = pltpu.make_async_copy(normed_hbm, rows_all, load.at[1])
    normed_load.start()
    normed_load.wait()

    def up_tile(index):
        at = tile_of(turned(index, model, leaving.shape[0]))
        active[at, :] = dot(rows_all[:, at], grad[...], ((0,), (0,))).astype(bf16)

    work_loop(model // TILE, up_tile, {1: [up_sum.begin]})
    late = [
        pltpu.make_async_copy(grad_packed_hbm, rows_all.at[:, 0:wide], load.at[2]),
        pltpu.make_async_copy(qkv_hbm, rows_all.at[:, wide : 2 * wide], load.at[3]),
        pltpu.make_async_copy(up_hbm, weight, load.at[4]),
    ]
    for copy in late:
        copy.start()
    up_events = up_sum.events()
    out_tokens.middle()
    events[-2]()
    out_tokens.final()
    inputs_load.wait()
    chunk = 32

    def both(ref, rows):
        return jnp.concatenate([ref[0, rows, :], ref[1, rows, :]], axis=1)

    def finish_output(index, carry):
        rows = span(index * chunk, chunk)
        output_ref[rows, :] = (
            away[0, rows, :].astype(f32)
            + both(slope, rows)
            + vectors_ref[2:3, :]
            + vectors_ref[3:4, :]
        ).astype(bf16)
        return carry

    lax.fori_loop(0, output_ref.shape[0] // chunk, finish_output, 0)
    out_tokens.end()
    near_by = ({"x": 1 - x}, {"y": 1 - y}, {"c": 1 - c})
    for index, device in enumerate(near_by):
        pl.semaphore_signal(free.at[index], inc=1, device_id=device, device_id_type=MESH)
    events[-1]()
    keeps[0].start()
    for copy in late:
        copy.wait()
    for index in range(3):
        pl.semaphore_wait(free.at[index], 1)
    work_loop(4, normed_tokens.give, {})
    work_loop(4, normed_tokens.take, {1: up_events[:1], 3: up_events[1:2]})
    normed_tokens.end_core()
    inputs_load.start()
    cot_load.start()
    packed_sum = jnp.zeros((1, wide), f32)

    def packed_tile(index, packed_sum):
        rows = rows_all[tile_of(index), :wide].astype(f32)
        return packed_sum + jnp.sum(rows, axis=0, keepdims=True)

    packed_sum = lax.fori_loop(0, count, packed_tile, packed_sum)
    for event in up_events[2:3]:
        event()
    normed_tokens.middle()
    for event in up_events[3:-2]:
        event()
    normed_tokens.final()
    inputs_load.wait()
    cot_load.wait()
    vector_sums[...] = jnp.zeros_like(vector_sums)
    gain = vectors_ref[0:1, :]

    def norm(index, carry):
        rows = span(index * chunk, chunk)
        source = away[0, rows, :].astype(f32)
        centered = source - jnp.mean(source, axis=1, keepdims=True)
        scale = lax.rsqrt(jnp.mean(centered * centered, axis=1, keepdims=True) + norm_eps)
        unit = centered * scale
        grads = both(slope, rows)
        cot = away[1, rows, :].astype(f32)
        vector_sums[0] += jnp.sum(grads * unit, axis=0, keepdims=True)
        vector_sums[1] += jnp.sum(grads, axis=0, keepdims=True)
        vector_sums[2] += jnp.sum(cot, axis=0, keepdims=True)
        grad_unit = grads * gain
        result = cot + scale * (
            grad_unit
            - jnp.mean(grad_unit, axis=1, keepdims=True)
            - unit * jnp.mean(grad_unit * unit, axis=1, keepdims=True)
        )
        half = result.shape[1] // 2
        slope[0, rows, :] = result[:, :half]
        slope[1, rows, :] = result[:, half:]
        return carry

    lax.fori_loop(0, output_ref.shape[0] // chunk, norm, 0)
    side = slope.shape[2]
    input_out = [
        pltpu.make_async_copy(
            slope.at[index], input_grad.at[:, index * side : (index + 1) * side], load.at[index + 4]
        )
        for index in (0, 1)
    ]
    for copy in input_out:
        copy.start()
    shards = steps * 2
    small_mine[...] = jnp.zeros_like(small_mine)
    vectors = [vector_sums[row] for row in range(3)]
    for shard in range(shards):
        for row in range(3):
            put_lines(
                small_mine, shard, row * small.norm_lines, vectors[row], shard * small.norm, small.norm
            )
    for part in range(steps):
        shard = x * steps + part
        for kind in range(3):
            start = kind * steps * small.bias + part * small.bias
            put_lines(small_mine, shard, 8 + kind, packed_sum, start, small.bias)
        put_lines(small_mine, shard, 11, hidden_sum, part * small.up, small.up)
    small_sums = SmallSum(steps, small_mine, small_ref, small_got, near_got, small_send, small_recv)
    small_sums.begin()
    down_sum.end()
    keeps[0].wait()
    up_events[-2]()
    small_sums.finish()
    up_events[-1]()
    keeps[1].start()
    for copy in input_out:
        copy.wait()
    normed_tokens.end()
    up_sum.end()
    keeps[1].wait()


def back(
    part,
    carry,
    cot,
    down,
    slope,
    attn,
    active,
    dense,
    normed,
    grad_packed,
    qkv,
    up,
    inputs,
    cot_own,
    vectors,
    small,
    steps,
):
    tokens, model = cot.shape
    hidden = down.shape[1]
    rows = tokens // 8
    depth = model // (2 * steps)
    shards = 2 * steps
    got = max(steps - 1, 1)
    anywhere = pl.BlockSpec(memory_space=pl.ANY)
    whole = pl.BlockSpec(memory_space=pltpu.VMEM)
    dma = pltpu.SemaphoreType.DMA
    half = pltpu.VMEM((2, rows // 2, model), bf16)
    return pl.pallas_call(
        partial(back_kernel, steps, small),
        in_specs=[anywhere] * 14 + [whole],
        out_specs=[anywhere] * 4 + [whole, anywhere, whole],
        out_shape=[
            jax.ShapeDtypeStruct((depth, hidden), f32),
            jax.ShapeDtypeStruct((depth, hidden), bf16),
            jax.ShapeDtypeStruct((depth, hidden), f32),
            jax.ShapeDtypeStruct((depth, hidden), bf16),
            jax.ShapeDtypeStruct((rows, model), bf16),
            jax.ShapeDtypeStruct((rows, model), f32),
            jax.ShapeDtypeStruct((16, 128), f32),
        ],
        scratch_shapes=[
            pltpu.VMEM((tokens, model), bf16),
            pltpu.VMEM((model, hidden), bf16),
            pltpu.VMEM((2, TILE, hidden), f32),
            pltpu.VMEM((tokens, hidden), bf16),
            pltpu.VMEM(attn.shape, bf16),
            pltpu.VMEM((tokens, hidden), bf16),
            pltpu.VMEM(dense.shape, bf16),
            pltpu.VMEM((4, rows, model), bf16),
            pltpu.VMEM((4, rows, model), bf16),
            half,
            half,
            half,
            dma((2, 10)),
            dma((2, 10)),
            pltpu.SemaphoreType.REGULAR((3,)),
            pltpu.VMEM((model, hidden), bf16),
            pltpu.VMEM((steps + 1, 2 * depth, hidden), bf16),
            pltpu.VMEM((steps + 1, 2 * depth, hidden), bf16),
            pltpu.VMEM((depth, hidden), f32),
            pltpu.VMEM((depth, hidden), bf16),
            dma((2, 2)),
            dma((2, got * 4)),
            dma((2, got * 4)),
            dma((9,)),
            dma((2,)),
            pltpu.VMEM((3, 1, model), f32),
            pltpu.VMEM((shards, 16, 128), f32),
            pltpu.VMEM((shards, 16, 128), f32),
            pltpu.VMEM((4, 8, 128), f32),
            dma((shards + 3,)),
            dma((shards + 3,)),
        ],
        cost_estimate=pl.CostEstimate(flops=5 * 10**10, bytes_accessed=2**27, transcendentals=0),
        compiler_params=pltpu.CompilerParams(
            collective_id=4, has_side_effects=True, vmem_limit_bytes=60 * 2**20
        ),
    )(
        part,
        carry,
        cot,
        down,
        slope,
        attn,
        active,
        dense,
        normed,
        grad_packed,
        qkv,
        up,
        inputs,
        cot_own,
        vectors,
    )


def adam(weight, grad, first, second, rate, decay):
    first_new = beta_one * first + (1.0 - beta_one) * grad
    second_new = beta_two * second + (1.0 - beta_two) * grad * grad
    scaled_first = first_new * (1.0 / (1.0 - beta_one**STEP))
    scaled_second = second_new * (1.0 / (1.0 - beta_two**STEP))
    weight_new = weight - rate * (
        scaled_first / (jnp.sqrt(scaled_second) + epsilon) + decay * weight
    )
    return (grad, weight_new, first_new, second_new)


def update_kernel(sizes, *refs):
    x = lax.axis_index("x")
    ins, outs = list(refs[:32]), list(refs[32:])
    for source, target in zip(ins[:2], outs[:2]):
        target[...] = source[...]
    ins, outs = ins[2:], outs[2:]

    def halves(kept, swapped):
        kept, swapped = kept, swapped.astype(f32)
        left = jnp.where(x == 0, kept, swapped)
        return left, jnp.where(x == 0, swapped, kept)

    def put(at, grad, rate, decay, index=()):
        weight, first, second = (ref[index] if index else ref[...] for ref in ins[at : at + 3])
        for ref, value in zip(outs, adam(weight, grad, first, second, rate, decay)):
            if index:
                ref[index] = value
            else:
                ref[...] = value

    kept, swapped = ins[0], ins[1]
    width = kept.shape[1] // 3
    for kind in range(3):
        cut = slice(kind * width, (kind + 1) * width)
        for side, grad in enumerate(halves(kept[:, cut], swapped[:, cut])):
            at = (kind, slice(None), slice(side * width, (side + 1) * width))
            put(2, grad, 0.02, 0.1, at)
    ins, outs = ins[5:], outs[4:]
    for _ in range(3):
        kept, swapped = ins[0], ins[1]
        width = kept.shape[1]
        for side, grad in enumerate(halves(kept[...], swapped[...])):
            put(2, grad, 0.02, 0.1, (slice(None), slice(side * width, (side + 1) * width)))
        ins, outs = ins[5:], outs[4:]

    @pl.when(pl.program_id(0) == 0)
    def _():
        nonlocal ins, outs
        small = ins[0][...]
        ins = ins[1:]
        put(0, small[8:11, : sizes.bias], 0.2, 0.0)
        ins, outs = ins[3:], outs[4:]
        across = min(128, sizes.up)
        put(0, small[11 : 11 + sizes.up // across, :across], 0.2, 0.0)
        ins, outs = ins[3:], outs[4:]
        lines = sizes.norm_lines
        rows = []
        for row in (0, 1, 2, 2):
            cuts = [small[row * lines + k : row * lines + k + 1, : sizes.across] for k in range(lines)]
            rows.append(jnp.concatenate(cuts, axis=1))
        put(0, jnp.concatenate(rows, axis=0), 0.2, 0.0)


def update(final, large, small, sizes):
    depth = large[0][0].shape[0]
    height = min(64, depth)

    def spec(part):
        if part.ndim == 3:
            return pl.BlockSpec((3, height, part.shape[2]), lambda i: (0, i, 0))
        return pl.BlockSpec((height, part.shape[1]), lambda i: (i, 0))

    def fixed(part):
        return pl.BlockSpec(part.shape, lambda i: (0, 0))

    def share(part):
        return pl.BlockSpec((part.shape[0] * height // depth, part.shape[1]), lambda i: (i, 0))

    args = [*final, *(part for group in large for part in group), small[0]]
    in_specs = [share(part) for part in final]
    in_specs += [spec(part) for part in args[2:-1]] + [fixed(small[0])]
    out_specs = [share(part) for part in final]
    out_shape = [jax.ShapeDtypeStruct(part.shape, part.dtype) for part in final]
    for group in large:
        out_specs += [spec(group[2])] * 4
        out_shape += [jax.ShapeDtypeStruct(group[2].shape, f32)] * 4
    for group in small[1:]:
        args += list(group)
        in_specs += [fixed(part) for part in group]
        out_specs += [fixed(group[0])] * 4
        out_shape += [jax.ShapeDtypeStruct(group[0].shape, f32)] * 4
    return pl.pallas_call(
        partial(update_kernel, sizes),
        grid=(depth // height,),
        in_specs=in_specs,
        out_specs=out_specs,
        out_shape=out_shape,
        cost_estimate=pl.CostEstimate(flops=3 * 10**7, bytes_accessed=5 * 10**7, transcendentals=0),
        compiler_params=pltpu.CompilerParams(vmem_limit_bytes=60 * 2**20),
    )(*args)


def on_device(
    inputs,
    cotangent,
    qkv_weight,
    qkv_first,
    qkv_second,
    dense_weight,
    dense_first,
    dense_second,
    up_weight,
    up_first,
    up_second,
    down_weight,
    down_first,
    down_second,
    qkv_bias,
    qkv_bias_first,
    qkv_bias_second,
    up_bias,
    up_bias_first,
    up_bias_second,
    norm_vectors,
    norm_first,
    norm_second,
):
    steps = lax.axis_size("z")
    shards = steps * lax.axis_size("x")
    z, x, y, c = (lax.axis_index(name) for name in ("z", "x", "y", "c"))
    rows, model = inputs.shape
    depth = qkv_weight.shape[0]
    own_bias = qkv_bias.shape[1]
    own_up = up_bias.shape[0]
    own_norm = norm_vectors.shape[1]

    sizes = SmallSizes(own_norm, own_bias, own_up)

    def in_rows(part):
        return part.reshape(-1, min(128, own_up))

    kinds_first = (1, 0, 2)
    qkv_parts = [part.transpose(kinds_first) for part in (qkv_weight, qkv_first, qkv_second)]
    (
        vectors,
        attn,
        grad_packed,
        normed_all,
        grad_all,
        qkv_full,
        dense_full,
        up_full,
        down_full,
        active,
        slope,
        down_part,
        carry,
        qkv_kept,
        qkv_swapped,
        dense_kept,
        dense_swapped,
    ) = front(
        norm_vectors,
        qkv_bias,
        in_rows(up_bias),
        inputs,
        cotangent,
        rope_tables(),
        qkv_parts[0],
        dense_weight,
        up_weight,
        down_weight,
        sizes,
        steps,
    )
    (
        down_kept,
        down_swapped,
        up_kept,
        up_swapped,
        output,
        input_grad,
        small_sums,
    ) = back(
        down_part,
        carry,
        grad_all,
        down_full,
        slope,
        attn,
        active,
        dense_full,
        normed_all,
        grad_packed,
        qkv_full,
        up_full,
        inputs,
        cotangent,
        vectors,
        sizes,
        steps,
    )

    large = (
        (qkv_kept, qkv_swapped, *qkv_parts),
        (dense_kept, dense_swapped, dense_weight, dense_first, dense_second),
        (up_kept, up_swapped, up_weight, up_first, up_second),
        (down_kept, down_swapped, down_weight, down_first, down_second),
    )
    little = (
        small_sums,
        (qkv_bias, qkv_bias_first, qkv_bias_second),
        tuple(in_rows(part) for part in (up_bias, up_bias_first, up_bias_second)),
        (norm_vectors, norm_first, norm_second),
    )
    new = list(update((output, input_grad), large, little, sizes))
    new[2:6] = [part.transpose(kinds_first) for part in new[2:6]]
    new[22:26] = [part.reshape(-1) for part in new[22:26]]
    return tuple(new)


def solution(mesh):
    data, tensor = mesh.shape["dp"], mesh.shape["tensor"]
    fine = Mesh(mesh.devices.reshape(data // 2, 2, tensor // 2, 2), ("z", "x", "y", "c"))
    dp, tp = ("z", "x"), ("y", "c")
    tokens = P(dp + tp, None)
    cube = P(dp, None, tp)
    matrix = P(dp, tp)
    bias_wide, bias, norm = P(None, tp + dp), P(tp + dp), P(None, dp)
    in_specs = (
        (tokens,) * 2
        + (cube,) * 3
        + (matrix,) * 9
        + (bias_wide,) * 3
        + (bias,) * 3
        + (norm,) * 3
    )
    out_specs = (
        (tokens,) * 2
        + (cube,) * 4
        + (matrix,) * 12
        + (bias_wide,) * 4
        + (bias,) * 4
        + (norm,) * 4
    )
    return jax.shard_map(
        on_device, mesh=fine, in_specs=in_specs, out_specs=out_specs, check_vma=False
    )
```
